32 devices in a mesh: wall: 2 (over x), span: 4 (over y, core), chord: 4 (over z).
Axes of the slice: x: 2, y: 2, z: 4, core: 2. Of those that a mesh axis runs over, the one named last changes fastest.
Arguments:
- source: float32 [4, 8, 8, 4, 320], P('span', 'chord', 'wall'), may hold values from -1.8 to 1.8
- adjoint_start: float32 [4, 8, 8, 4, 320], P('span', 'chord', 'wall'), may hold values from -6 to 6
- pivot_inverse: float32 [4, 8, 8, 320, 320], P('span', 'chord', 'wall'), as said below
- upper_block: float32 [4, 8, 8, 320, 320], P('span', 'chord', 'wall'), may hold values from -0.3125 to 0.3125
- lower_block: float32 [4, 8, 8, 320, 320], P('span', 'chord', 'wall'), may hold values from -0.3125 to 0.3125
- face_coupling: float32 [4, 80, 320], replicated, may hold values from -0.03125 to 0.03125
Outputs:
- adjoint: float32 [4, 8, 8, 4, 320], P('span', 'chord', 'wall')
The draws below stay inside these ranges and needn't reach their ends.
Inputs may be any that keep to these rules, and one draw needn't show every extreme that they name: `pivot_inverse`: each block equals 0.9 times the identity plus independent noise of root-mean-square 0.3 times 320 ** -0.5 an entry.
All inputs are finite; a program needn't handle non-finite values.
Results may differ from the reference program's by a relative error of at most 0.0003.
Values sent between devices are 32-bit elements; how exact they have to be, the bound alone decides.
A program may use at most 128 MiB of HBM per device.

```python
import math
import jax
import jax.numpy as jnp
from jax import lax

NV = 5
P1 = 4
B = 320
FACE = 80
OBJ = 4
SWEEPS = 2
NE = 8
NSP = 4
NCH = 8


def draw_pivot_inverse(key, part):
    shape = (NSP, NCH, NE, B, B)
    eye_table = (lax.broadcasted_iota(jnp.int32, (B, B), 0) == lax.broadcasted_iota(jnp.int32, (B, B), 1)).astype(jnp.float32)
    noise = jax.random.normal(key, shape, jnp.float32) * (0.3 / math.sqrt(B))
    return 0.9 * eye_table + noise


def block_levels(stream_key, dims, cuts, low, high):
    gain = 1.0
    for axis_at, blocks in cuts:
        draws = jax.random.uniform(jax.random.fold_in(jax.random.fold_in(stream_key, 6), axis_at), (blocks,), jnp.float32, low / len(cuts), high / len(cuts))
        gain = gain * jnp.repeat(jnp.exp(draws), dims[axis_at] // blocks).reshape((-1,) + (1,) * (len(dims) - 1 - axis_at))
    return gain


def normal_values(key, dims, deviation, reach, cuts=(), held_as=jnp.bfloat16):
    entries = deviation * jax.random.normal(key, dims, jnp.float32)
    if cuts:
        entries = entries * block_levels(key, dims, cuts, -0.22, 0.18)
    return jnp.clip(entries, -reach, reach).astype(held_as)


def setup_inputs(seed: int = 0) -> dict:
    splits = jax.random.split(jax.random.key(seed), 7)
    return {
        "source": normal_values(splits[0], (NSP, NCH, NE, OBJ, B), 0.3, 1.8, ((0, 4), (1, 4), (2, 2)), jnp.float32),
        "adjoint_start": normal_values(splits[1], (NSP, NCH, NE, OBJ, B), 1.0, 6.0, ((0, 4), (1, 4), (2, 2)), jnp.float32),
        "pivot_inverse": draw_pivot_inverse(jax.random.fold_in(splits[6], 71), 0),
        "upper_block": normal_values(splits[3], (NSP, NCH, NE, B, B), B ** -0.5, 0.3125, ((0, 4), (1, 4), (2, 2)), jnp.float32),
        "lower_block": normal_values(splits[4], (NSP, NCH, NE, B, B), (B + B // 8) ** -0.5, 0.3125, ((0, 4), (1, 4), (2, 2)), jnp.float32),
        "face_coupling": normal_values(splits[5], (4, FACE, B), (400 * FACE) ** -0.5, 0.03125, (), jnp.float32),
    }


def face_traces(values):
    lead = values.shape[:4]
    shaped = values.reshape(lead + (NV, P1, P1, P1))
    flat = lead + (FACE,)
    return (shaped[..., :, 0, :, :].reshape(flat), shaped[..., :, P1 - 1, :, :].reshape(flat),
            shaped[..., :, :, 0, :].reshape(flat), shaped[..., :, :, P1 - 1, :].reshape(flat))


def from_next(values, axis):
    rest = lax.slice_in_dim(values, 1, values.shape[axis], axis=axis)
    blank = jnp.zeros_like(lax.slice_in_dim(values, 0, 1, axis=axis))
    return jnp.concatenate([rest, blank], axis=axis)


def from_prev(values, axis):
    rest = lax.slice_in_dim(values, 0, values.shape[axis] - 1, axis=axis)
    blank = jnp.zeros_like(lax.slice_in_dim(values, 0, 1, axis=axis))
    return jnp.concatenate([blank, rest], axis=axis)


def reference(source, adjoint_start, pivot_inverse, upper_block, lower_block, face_coupling):
    precise = lax.Precision.HIGHEST
    adjoint = adjoint_start
    pivots = jnp.moveaxis(pivot_inverse, 2, 0)
    uppers = jnp.moveaxis(upper_block, 2, 0)
    lowers = jnp.moveaxis(lower_block, 2, 0)
    for sweep_index in range(SWEEPS):
        low_span, high_span, low_chord, high_chord = face_traces(adjoint)
        neighbours = (from_next(low_span, 0), from_prev(high_span, 0),
                      from_next(low_chord, 1), from_prev(high_chord, 1))
        lateral = jnp.zeros_like(source)
        for which in range(4):
            lateral = lateral + jnp.einsum('scerf,fb->scerb', neighbours[which], face_coupling[which], precision=precise)
        right_side = jnp.moveaxis(source - lateral, 2, 0)

        def forward_step(carried, pieces):
            right_piece, pivot_piece, upper_piece = pieces
            value = jnp.einsum('scrb,scbk->scrk', right_piece - carried, pivot_piece, precision=precise)
            return jnp.einsum('scrb,scbk->scrk', value, upper_piece, precision=precise), value

        start = jnp.zeros(right_side.shape[1:], jnp.float32)
        unused, forward = lax.scan(forward_step, start, (right_side, pivots, uppers))

        def backward_step(carried, pieces):
            forward_piece, lower_piece = pieces
            value = forward_piece - carried
            return jnp.einsum('scrb,scbk->scrk', value, lower_piece, precision=precise), value

        unused, result = lax.scan(backward_step, start, (forward, lowers), reverse=True)
        adjoint = jnp.moveaxis(result, 0, 2)
    return adjoint
```

```python
import functools
import jax
import jax.numpy as jnp
from jax import lax
from jax.experimental import pallas as pl
from jax.experimental.pallas import tpu as pltpu
from jax.sharding import PartitionSpec as P

NV = 5
P1 = 4
SWEEPS = 2
AXES = ("wall", "span", "chord")


def kernel(sizes, src, adj, piv, upp, low, face, out,
           wf, wh, wl, ef, eh, el, zs, rs, fw, ab, sf, sb, rf, rb,
           r_sn, r_sp, r_cn, r_cp, msem, wsend, wrecv, fsend, frecv):
    lines, elements, obj, width = src.shape[1:]
    rows = lines * elements * obj
    place = {a: lax.axis_index(a) for a in AXES}
    f32, bf16 = jnp.float32, jnp.bfloat16

    def has(axis, step):
        return place[axis] < sizes[axis] - 1 if step > 0 else place[axis] > 0

    def to(axis, step):
        return {axis: jnp.clip(place[axis] + step, 0, sizes[axis] - 1)}

    def load(kind, ref, e):
        return pltpu.make_async_copy(ref.at[0, :, e], wf.at[kind, e], msem.at[kind, e])

    for e in range(elements):
        load(0, piv, e).start()
        load(1, upp, e).start()
    for e in reversed(range(elements)):
        load(2, low, e).start()

    barrier = pltpu.get_barrier_semaphore()
    sides = [(a, s) for a in AXES for s in (1, -1)]
    for axis, step in sides:
        @pl.when(has(axis, step))
        def _():
            pl.semaphore_signal(barrier, inc=1, device_id=to(axis, step), device_id_type=pl.DeviceIdType.MESH)
    pl.semaphore_wait(barrier, sum(has(axis, step).astype(jnp.int32) for axis, step in sides))

    def face_copies(sweep):
        whole = adj.at[0] if sweep == 0 else ab
        parts = (
            ("span", -1, whole, r_sn),
            ("span", 1, whole, r_sp),
            ("chord", -1, whole.at[0], r_cn),
            ("chord", 1, whole.at[lines - 1], r_cp),
        )
        return [
            (axis, step, pltpu.make_async_remote_copy(
                src_ref=a, dst_ref=b.at[sweep], send_sem=fsend.at[sweep, i], recv_sem=frecv.at[sweep, i],
                device_id=to(axis, step), device_id_type=pl.DeviceIdType.MESH))
            for i, (axis, step, a, b) in enumerate(parts)
        ]

    def send_faces(sweep):
        for axis, step, copy in face_copies(sweep):
            @pl.when(has(axis, step))
            def _():
                copy.start()

    def wait_faces(sweep):
        for axis, step, copy in face_copies(sweep):
            @pl.when(has(axis, -step))
            def _():
                copy.wait_recv()

    def wall_copy(sweep, way):
        a, b = (sf, rf) if way > 0 else (sb, rb)
        i = 0 if way > 0 else 1
        return pltpu.make_async_remote_copy(
            src_ref=a.at[sweep], dst_ref=b.at[sweep], send_sem=wsend.at[sweep, i], recv_sem=wrecv.at[sweep, i],
            device_id=to("wall", way), device_id_type=pl.DeviceIdType.MESH)

    def split_block(kind, ref, e):
        load(kind, ref, e).wait()
        for line in range(lines):
            full = wf[kind, e, line]
            high = full.astype(bf16)
            wh[kind, e, line] = high
            wl[kind, e, line] = (full - high.astype(f32)).astype(bf16)

    def pieces(x):
        high = x.astype(bf16).astype(f32)
        return jnp.concatenate([high, x - high], axis=0).astype(bf16)

    def times(x, high, low_):
        n = x.shape[0]
        both = pieces(x)
        y = jnp.dot(both, high, preferred_element_type=f32) + jnp.dot(both, low_, preferred_element_type=f32)
        return y[:n] + y[n:]

    send_faces(0)

    for axis, step, ref in (("span", 1, r_sn), ("span", -1, r_sp), ("chord", 1, r_cn), ("chord", -1, r_cp)):
        @pl.when(jnp.logical_not(has(axis, step)))
        def _():
            ref[...] = jnp.zeros_like(ref)

    @pl.when(jnp.logical_not(has("wall", -1)))
    def _():
        rf[...] = jnp.zeros_like(rf)

    @pl.when(jnp.logical_not(has("wall", 1)))
    def _():
        rb[...] = jnp.zeros_like(rb)

    ef[...] = jnp.zeros_like(ef)
    run = P1 * P1
    for v in range(NV):
        top = v * P1 * run
        ef[0, top:top + run, :] = face[0, v * run:(v + 1) * run, :]
        ef[0, top + 3 * run:top + 4 * run, :] = face[1, v * run:(v + 1) * run, :]
    for g in range(NV * P1):
        ef[1, g * run:g * run + P1, :] = face[2, g * P1:(g + 1) * P1, :]
        ef[1, g * run + 3 * P1:(g + 1) * run, :] = face[3, g * P1:(g + 1) * P1, :]
    for d in range(2):
        full = ef[d]
        high = full.astype(bf16)
        eh[d] = high
        el[d] = (full - high.astype(f32)).astype(bf16)

    for e in range(elements):
        split_block(0, piv, e)
        split_block(1, upp, e)

    lane = lax.broadcasted_iota(jnp.int32, (obj, width), 1)
    span_node = (lane >> 4) & 3
    chord_node = (lane >> 2) & 3

    for sweep in range(SWEEPS):
        wait_faces(sweep)
        for line in range(lines):
            for e in range(elements):
                at = (line * elements + e) * obj
                now = adj.at[0] if sweep == 0 else ab
                zs[0, at:at + obj, :] = jnp.where(
                    span_node == 0, r_sn[sweep, line, e], jnp.where(span_node == 3, r_sp[sweep, line, e], 0.0))
                above = now[line + 1, e] if line + 1 < lines else r_cn[sweep, e]
                below = now[line - 1, e] if line > 0 else r_cp[sweep, e]
                zs[1, at:at + obj, :] = jnp.where(
                    chord_node == 0, above, jnp.where(chord_node == 3, below, 0.0))
        rs[...] = times(zs[0], eh[0], el[0]) + times(zs[1], eh[1], el[1])

        if sweep == 0:
            @pl.when(has("wall", -1))
            def _():
                for e in reversed(range(elements)):
                    split_block(2, low, e)

        @pl.when(has("wall", -1))
        def _():
            wall_copy(sweep, 1).wait_recv()

        carried = [rf[sweep, line] for line in range(lines)]
        for e in range(elements):
            for line in range(lines):
                at = (line * elements + e) * obj
                value = times(src[0, line, e] - rs[at:at + obj, :] - carried[line], wh[0, e, line], wl[0, e, line])
                fw[line, e] = value
                carried[line] = times(value, wh[1, e, line], wl[1, e, line])
        for line in range(lines):
            sf[sweep, line] = carried[line]

        @pl.when(has("wall", 1))
        def _():
            wall_copy(sweep, 1).start()

        if sweep == 0:
            @pl.when(jnp.logical_not(has("wall", -1)))
            def _():
                for e in reversed(range(elements)):
                    split_block(2, low, e)

        @pl.when(has("wall", 1))
        def _():
            wall_copy(sweep, -1).wait_recv()

        last = sweep == SWEEPS - 1
        carried = [rb[sweep, line] for line in range(lines)]
        for e in reversed(range(elements)):
            for line in range(lines):
                value = fw[line, e] - carried[line]
                if last:
                    out[0, line, e] = value
                else:
                    ab[line, e] = value
                carried[line] = times(value, wh[2, e, line], wl[2, e, line])
        for line in range(lines):
            sb[sweep, line] = carried[line]

        @pl.when(has("wall", -1))
        def _():
            wall_copy(sweep, -1).start()

        if not last:
            send_faces(sweep + 1)

    for sweep in range(SWEEPS):
        for axis, step, copy in face_copies(sweep):
            @pl.when(has(axis, step))
            def _():
                copy.wait_send()
        for way in (1, -1):
            @pl.when(has("wall", way))
            def _():
                wall_copy(sweep, way).wait_send()


def local(sizes, source, adjoint_start, pivot_inverse, upper_block, lower_block, face_coupling):
    lines, elements, obj, width = source.shape[1:]
    f32, bf16 = jnp.float32, jnp.bfloat16
    vmem = pl.BlockSpec(memory_space=pltpu.VMEM)
    anywhere = pl.BlockSpec(memory_space=pl.ANY)
    rows = lines * elements * obj
    edge = pltpu.VMEM((SWEEPS, lines, obj, width), f32)
    blocks = (3, elements, lines, width, width)
    return pl.pallas_call(
        functools.partial(kernel, sizes),
        out_shape=jax.ShapeDtypeStruct(source.shape, f32),
        in_specs=[vmem, vmem, anywhere, anywhere, anywhere, vmem],
        out_specs=vmem,
        scratch_shapes=[
            pltpu.VMEM(blocks, f32), pltpu.VMEM(blocks, bf16), pltpu.VMEM(blocks, bf16),
            pltpu.VMEM((2, width, width), f32), pltpu.VMEM((2, width, width), bf16),
            pltpu.VMEM((2, width, width), bf16),
            pltpu.VMEM((2, rows, width), f32), pltpu.VMEM((rows, width), f32),
            pltpu.VMEM((lines, elements, obj, width), f32), pltpu.VMEM((lines, elements, obj, width), f32),
            edge, edge, edge, edge,
            pltpu.VMEM((SWEEPS, lines, elements, obj, width), f32),
            pltpu.VMEM((SWEEPS, lines, elements, obj, width), f32),
            pltpu.VMEM((SWEEPS, elements, obj, width), f32),
            pltpu.VMEM((SWEEPS, elements, obj, width), f32),
            pltpu.SemaphoreType.DMA((3, elements)),
            pltpu.SemaphoreType.DMA((SWEEPS, 2)), pltpu.SemaphoreType.DMA((SWEEPS, 2)),
            pltpu.SemaphoreType.DMA((SWEEPS, 4)), pltpu.SemaphoreType.DMA((SWEEPS, 4)),
        ],
        compiler_params=pltpu.CompilerParams(
            collective_id=0, has_side_effects=True, vmem_limit_bytes=60 * 1024 * 1024),
    )(source, adjoint_start, pivot_inverse, upper_block, lower_block, face_coupling)


def solution(mesh):
    spec = P("span", "chord", "wall", None, None)
    return jax.shard_map(
        functools.partial(local, dict(mesh.shape)),
        mesh=mesh,
        in_specs=(spec, spec, spec, spec, spec, P()),
        out_specs=spec,
        check_vma=False,
    )
```

```python
import functools
import jax
import jax.numpy as jnp
from jax import lax
from jax.experimental import pallas as pl
from jax.experimental.pallas import tpu as pltpu
from jax.sharding import PartitionSpec as P

NV = 5
P1 = 4
SWEEPS = 2
AXES = ("wall", "span", "chord")


def kernel(sizes, src_in, adj_in, piv, upp, low, face_in, out,
           src, adj, face, qh, ql, th, tl, small, wf, wh, wl, ef, eh, el, zs, rs, fw, ab, sf, sb, rf, rb,
           r_sn, r_sp, r_cn, r_cp, msem, wsend, wrecv, fsend, frecv):
    lines, elements, obj, width = src_in.shape[1:]
    rows = lines * elements * obj
    place = {a: lax.axis_index(a) for a in AXES}
    f32, bf16 = jnp.float32, jnp.bfloat16

    def has(axis, step):
        return place[axis] < sizes[axis] - 1 if step > 0 else place[axis] > 0

    def to(axis, step):
        return {axis: jnp.clip(place[axis] + step, 0, sizes[axis] - 1)}

    def load(kind, ref, e):
        return pltpu.make_async_copy(ref.at[0, :, e], wf.at[kind, e], msem.at[kind, e])

    minor = [
        pltpu.make_async_copy(a, b, small.at[i])
        for i, (a, b) in enumerate(((face_in, face), (adj_in, adj), (src_in, src)))
    ]
    for copy in minor:
        copy.start()
    for e in range(elements):
        load(0, piv, e).start()
        load(1, upp, e).start()
    for e in reversed(range(elements)):
        load(2, low, e).start()

    barrier = pltpu.get_barrier_semaphore()
    sides = [(a, s) for a in AXES for s in (1, -1)]
    for axis, step in sides:
        @pl.when(has(axis, step))
        def _():
            pl.semaphore_signal(barrier, inc=1, device_id=to(axis, step), device_id_type=pl.DeviceIdType.MESH)
    pl.semaphore_wait(barrier, sum(has(axis, step).astype(jnp.int32) for axis, step in sides))

    def face_copies(sweep, which=(0, 1)):
        whole = adj_in.at[0] if sweep == 0 else ab
        found = []
        for part, cut in enumerate((pl.ds(1, elements - 1), pl.ds(0, 1))):
            if part not in which:
                continue
            parts = (
                ("chord", -1, whole.at[0, cut], r_cn.at[sweep, cut]),
                ("chord", 1, whole.at[lines - 1, cut], r_cp.at[sweep, cut]),
                ("span", -1, whole.at[:, cut], r_sn.at[sweep, :, cut]),
                ("span", 1, whole.at[:, cut], r_sp.at[sweep, :, cut]),
            )
            for i, (axis, step, a, b) in enumerate(parts):
                found.append((part, axis, step, pltpu.make_async_remote_copy(
                    src_ref=a, dst_ref=b, send_sem=fsend.at[sweep, part, i], recv_sem=frecv.at[sweep, part, i],
                    device_id=to(axis, step), device_id_type=pl.DeviceIdType.MESH)))
        return found

    def send_faces(sweep, which):
        for part, axis, step, copy in face_copies(sweep, (which,)):
            @pl.when(has(axis, step))
            def _():
                copy.start()

    def wait_faces(sweep):
        for part, axis, step, copy in face_copies(sweep):
            @pl.when(has(axis, -step))
            def _():
                copy.wait_recv()

    def wall_copy(sweep, way):
        a, b = (sf, rf) if way > 0 else (sb, rb)
        i = 0 if way > 0 else 1
        return pltpu.make_async_remote_copy(
            src_ref=a.at[sweep], dst_ref=b.at[sweep], send_sem=wsend.at[sweep, i], recv_sem=wrecv.at[sweep, i],
            device_id=to("wall", way), device_id_type=pl.DeviceIdType.MESH)

    def split_block(kind, ref, e):
        load(kind, ref, e).wait()
        for line in range(lines):
            full = wf[kind, e, line]
            high = full.astype(bf16)
            wh[kind, e, line] = high
            wl[kind, e, line] = (full - high.astype(f32)).astype(bf16)

    def pieces(x):
        high = x.astype(bf16).astype(f32)
        return jnp.concatenate([high, x - high], axis=0).astype(bf16)

    def times(x, high, low_):
        n = x.shape[0]
        both = pieces(x)
        y = jnp.dot(both, high, preferred_element_type=f32) + jnp.dot(both, low_, preferred_element_type=f32)
        return y[:n] + y[n:]

    def product(ah, al, bh, bl):
        dot = functools.partial(jnp.dot, preferred_element_type=f32)
        return dot(ah, bh) + dot(al, bh) + dot(ah, bl)

    def halves(full):
        high = full.astype(bf16)
        return high, (full - high.astype(f32)).astype(bf16)

    def form_pairs(line, unused):
        for e in range(elements):
            qh[e, line], ql[e, line] = halves(
                product(wh[0, e, line], wl[0, e, line], wh[1, e, line], wl[1, e, line]))
        return unused

    start = 1 if elements > 1 else 0

    def begin_response(line, unused):
        e = elements - 1
        th[line], tl[line] = halves(-product(wh[0, e, line], wl[0, e, line], wh[2, e, line], wl[2, e, line]))
        return unused

    def form_response(line, unused):
        eye = (lax.broadcasted_iota(jnp.int32, (width, width), 0)
               == lax.broadcasted_iota(jnp.int32, (width, width), 1)).astype(f32)
        for e in reversed(range(start, elements - 1)):
            ah, al = halves(eye - product(wh[1, e, line], wl[1, e, line], th[line], tl[line]))
            ah, al = halves(product(wh[0, e, line], wl[0, e, line], ah, al))
            th[line], tl[line] = halves(-product(ah, al, wh[2, e, line], wl[2, e, line]))
        return unused

    send_faces(0, 0)
    send_faces(0, 1)

    for axis, step, ref in (("span", 1, r_sn), ("span", -1, r_sp), ("chord", 1, r_cn), ("chord", -1, r_cp)):
        @pl.when(jnp.logical_not(has(axis, step)))
        def _():
            ref[...] = jnp.zeros_like(ref)

    @pl.when(jnp.logical_not(has("wall", -1)))
    def _():
        rf[...] = jnp.zeros_like(rf)

    @pl.when(jnp.logical_not(has("wall", 1)))
    def _():
        rb[...] = jnp.zeros_like(rb)

    ef[...] = jnp.zeros_like(ef)
    minor[0].wait()
    run = P1 * P1
    for v in range(NV):
        top = v * P1 * run
        ef[0, top:top + run, :] = face[0, v * run:(v + 1) * run, :]
        ef[0, top + 3 * run:top + 4 * run, :] = face[1, v * run:(v + 1) * run, :]
    for g in range(NV * P1):
        ef[1, g * run:g * run + P1, :] = face[2, g * P1:(g + 1) * P1, :]
        ef[1, g * run + 3 * P1:(g + 1) * run, :] = face[3, g * P1:(g + 1) * P1, :]
    for d in range(2):
        full = ef[d]
        high = full.astype(bf16)
        eh[d] = high
        el[d] = (full - high.astype(f32)).astype(bf16)

    for e in range(elements):
        split_block(0, piv, e)
        split_block(1, upp, e)

    minor[1].wait()
    minor[2].wait()

    lane = lax.broadcasted_iota(jnp.int32, (obj, width), 1)
    span_node = (lane >> 4) & 3
    chord_node = (lane >> 2) & 3

    for sweep in range(SWEEPS):
        wait_faces(sweep)
        for line in range(lines):
            for e in range(elements):
                at = (line * elements + e) * obj
                now = adj.at[0] if sweep == 0 else ab
                zs[0, at:at + obj, :] = jnp.where(
                    span_node == 0, r_sn[sweep, line, e], jnp.where(span_node == 3, r_sp[sweep, line, e], 0.0))
                above = now[line + 1, e] if line + 1 < lines else r_cn[sweep, e]
                below = now[line - 1, e] if line > 0 else r_cp[sweep, e]
                zs[1, at:at + obj, :] = jnp.where(
                    chord_node == 0, above, jnp.where(chord_node == 3, below, 0.0))
        rs[...] = times(zs[0], eh[0], el[0]) + times(zs[1], eh[1], el[1])

        last = sweep == SWEEPS - 1

        def right(line, e):
            at = (line * elements + e) * obj
            return src[0, line, e] - rs[at:at + obj, :]

        def forward(carried, final=True, first=0, end=elements):
            carried = list(carried)
            for e in range(first, end):
                for line in range(lines):
                    value = times(right(line, e) - carried[line], wh[0, e, line], wl[0, e, line])
                    fw[line, e] = value
                    if final or e < end - 1:
                        carried[line] = times(value, wh[1, e, line], wl[1, e, line])
            return carried

        def backward(carried, store, final=True, first=0, end=elements):
            carried = list(carried)
            for e in reversed(range(first, end)):
                for line in range(lines):
                    value = fw[line, e] - carried[line]
                    if store:
                        if last:
                            out[0, line, e] = value
                        else:
                            ab[line, e] = value
                    if final or e > first:
                        carried[line] = times(value, wh[2, e, line], wl[2, e, line])
                if store and not last and e == 1:
                    send_faces(sweep + 1, 0)
            return carried

        def received(ref):
            return [ref[sweep, line] for line in range(lines)]

        def keep(ref, values):
            for line in range(lines):
                ref[sweep, line] = values[line]

        blank = [jnp.zeros((obj, width), f32)] * lines
        opening, closing = jnp.logical_not(has("wall", -1)), jnp.logical_not(has("wall", 1))
        middle = jnp.logical_and(has("wall", -1), has("wall", 1))

        def split_lower():
            for e in reversed(range(elements)):
                split_block(2, low, e)

        @pl.when(opening)
        def _():
            if sweep == 0:
                keep(sf, forward(blank))
            else:
                carried = list(blank)
                for e in range(elements):
                    for line in range(lines):
                        small_right = right(line, e) - carried[line]
                        rs[(line * elements + e) * obj:(line * elements + e + 1) * obj, :] = small_right
                        carried[line] = times(small_right, qh[e, line], ql[e, line])
                keep(sf, carried)

            @pl.when(has("wall", 1))
            def _():
                wall_copy(sweep, 1).start()

            if sweep == 0:
                split_lower()
                lax.fori_loop(0, lines, form_pairs, 0)
            else:
                for e in range(elements):
                    for line in range(lines):
                        at = (line * elements + e) * obj
                        fw[line, e] = times(rs[at:at + obj, :], wh[0, e, line], wl[0, e, line])

            @pl.when(has("wall", 1))
            def _():
                wall_copy(sweep, -1).wait_recv()

            backward(received(rb), True, False)
            if not last:
                send_faces(sweep + 1, 1)

        @pl.when(middle)
        def _():
            if sweep == 0:
                split_lower()
            wall_copy(sweep, 1).wait_recv()
            keep(sf, forward(received(rf)))
            wall_copy(sweep, 1).start()
            wall_copy(sweep, -1).wait_recv()
            keep(sb, backward(received(rb), True))
            wall_copy(sweep, -1).start()
            if not last:
                send_faces(sweep + 1, 1)

        @pl.when(jnp.logical_and(closing, has("wall", -1)))
        def _():
            if sweep == 0:
                split_lower()
                lax.fori_loop(0, lines, begin_response, 0)
                wall_copy(sweep, 1).wait_recv()
                forward(received(rf), False)
                keep(sb, backward(blank, True))
                wall_copy(sweep, -1).start()
                if not last:
                    send_faces(sweep + 1, 1)
                    lax.fori_loop(0, lines, form_response, 0)
            else:
                forward(blank, False, start)
                apart = backward(blank, False, True, start)
                wall_copy(sweep, 1).wait_recv()
                came = forward(received(rf), True, 0, start)
                back = [apart[line] + times(came[line], th[line], tl[line]) for line in range(lines)]
                keep(sb, backward(back, True, True, 0, start))
                wall_copy(sweep, -1).start()
                forward(came, False, start)
                backward(blank, True, False, start)
                if not last:
                    send_faces(sweep + 1, 1)

    for sweep in range(SWEEPS):
        for part, axis, step, copy in face_copies(sweep):
            @pl.when(has(axis, step))
            def _():
                copy.wait_send()
        for way in (1, -1):
            @pl.when(has("wall", way))
            def _():
                wall_copy(sweep, way).wait_send()


def local(sizes, source, adjoint_start, pivot_inverse, upper_block, lower_block, face_coupling):
    lines, elements, obj, width = source.shape[1:]
    f32, bf16 = jnp.float32, jnp.bfloat16
    vmem = pl.BlockSpec(memory_space=pltpu.VMEM)
    anywhere = pl.BlockSpec(memory_space=pl.ANY)
    rows = lines * elements * obj
    edge = pltpu.VMEM((SWEEPS, lines, obj, width), f32)
    blocks = (3, elements, lines, width, width)
    return pl.pallas_call(
        functools.partial(kernel, sizes),
        out_shape=jax.ShapeDtypeStruct(source.shape, f32),
        in_specs=[anywhere] * 6,
        out_specs=vmem,
        scratch_shapes=[
            pltpu.VMEM(source.shape, f32), pltpu.VMEM(source.shape, f32), pltpu.VMEM(face_coupling.shape, f32),
            pltpu.VMEM(blocks[1:], bf16), pltpu.VMEM(blocks[1:], bf16),
            pltpu.VMEM(blocks[2:], bf16), pltpu.VMEM(blocks[2:], bf16), pltpu.SemaphoreType.DMA((3,)),
            pltpu.VMEM(blocks, f32), pltpu.VMEM(blocks, bf16), pltpu.VMEM(blocks, bf16),
            pltpu.VMEM((2, width, width), f32), pltpu.VMEM((2, width, width), bf16),
            pltpu.VMEM((2, width, width), bf16),
            pltpu.VMEM((2, rows, width), f32), pltpu.VMEM((rows, width), f32),
            pltpu.VMEM((lines, elements, obj, width), f32), pltpu.VMEM((lines, elements, obj, width), f32),
            edge, edge, edge, edge,
            pltpu.VMEM((SWEEPS, lines, elements, obj, width), f32),
            pltpu.VMEM((SWEEPS, lines, elements, obj, width), f32),
            pltpu.VMEM((SWEEPS, elements, obj, width), f32),
            pltpu.VMEM((SWEEPS, elements, obj, width), f32),
            pltpu.SemaphoreType.DMA((3, elements)),
            pltpu.SemaphoreType.DMA((SWEEPS, 2)), pltpu.SemaphoreType.DMA((SWEEPS, 2)),
            pltpu.SemaphoreType.DMA((SWEEPS, 2, 4)), pltpu.SemaphoreType.DMA((SWEEPS, 2, 4)),
        ],
        compiler_params=pltpu.CompilerParams(
            collective_id=0, has_side_effects=True, vmem_limit_bytes=60 * 1024 * 1024),
    )(source, adjoint_start, pivot_inverse, upper_block, lower_block, face_coupling)


def solution(mesh):
    spec = P("span", "chord", "wall", None, None)
    return jax.shard_map(
        functools.partial(local, dict(mesh.shape)),
        mesh=mesh,
        in_specs=(spec, spec, spec, spec, spec, P()),
        out_specs=spec,
        check_vma=False,
    )
```

```python
import functools
import jax
import jax.numpy as jnp
from jax import lax
from jax.experimental import pallas as pl
from jax.experimental.pallas import tpu as pltpu
from jax.sharding import PartitionSpec as P

NV = 5
P1 = 4
SWEEPS = 2
AXES = ("wall", "span", "chord")


def kernel(sizes, src_in, adj_in, piv, upp, low, face_in, out,
           src, adj, face, qh, ql, th, tl, small, wf, wh, wl, ef, eh, el, zs, rs, fw, ab, sf, sb, rf, rb,
           r_sn, r_sp, r_cn, r_cp, msem, wsend, wrecv, fsend, frecv):
    lines, elements, obj, width = src_in.shape[1:]
    rows = lines * elements * obj
    place = {a: lax.axis_index(a) for a in AXES}
    f32, bf16 = jnp.float32, jnp.bfloat16

    def has(axis, step):
        return place[axis] < sizes[axis] - 1 if step > 0 else place[axis] > 0

    def to(axis, step):
        return {axis: jnp.clip(place[axis] + step, 0, sizes[axis] - 1)}

    def load(kind, ref, e):
        return pltpu.make_async_copy(ref.at[0, :, e], wf.at[kind, e], msem.at[kind, e])

    minor = [
        pltpu.make_async_copy(a, b, small.at[i])
        for i, (a, b) in enumerate(((face_in, face), (adj_in, adj), (src_in, src)))
    ]
    for copy in minor:
        copy.start()
    for e in range(elements):
        load(0, piv, e).start()
        load(1, upp, e).start()
    for e in reversed(range(elements)):
        load(2, low, e).start()

    barrier = pltpu.get_barrier_semaphore()
    sides = [(a, s) for a in AXES for s in (1, -1)]
    for axis, step in sides:
        @pl.when(has(axis, step))
        def _():
            pl.semaphore_signal(barrier, inc=1, device_id=to(axis, step), device_id_type=pl.DeviceIdType.MESH)
    pl.semaphore_wait(barrier, sum(has(axis, step).astype(jnp.int32) for axis, step in sides))

    def face_copies(sweep, which=(0, 1)):
        whole = adj_in.at[0] if sweep == 0 else ab
        found = []
        for part, cut in enumerate((pl.ds(1, elements - 1), pl.ds(0, 1))):
            if part not in which:
                continue
            parts = (
                ("chord", -1, whole.at[0, cut], r_cn.at[sweep, cut]),
                ("chord", 1, whole.at[lines - 1, cut], r_cp.at[sweep, cut]),
                ("span", -1, whole.at[:, cut], r_sn.at[sweep, :, cut]),
                ("span", 1, whole.at[:, cut], r_sp.at[sweep, :, cut]),
            )
            for i, (axis, step, a, b) in enumerate(parts):
                found.append((part, axis, step, pltpu.make_async_remote_copy(
                    src_ref=a, dst_ref=b, send_sem=fsend.at[sweep, part, i], recv_sem=frecv.at[sweep, part, i],
                    device_id=to(axis, step), device_id_type=pl.DeviceIdType.MESH)))
        return found

    def send_faces(sweep, which):
        for part, axis, step, copy in face_copies(sweep, (which,)):
            @pl.when(has(axis, step))
            def _():
                copy.start()

    def wait_faces(sweep):
        for part, axis, step, copy in face_copies(sweep):
            @pl.when(has(axis, -step))
            def _():
                copy.wait_recv()

    def wall_copy(sweep, way):
        a, b = (sf, rf) if way > 0 else (sb, rb)
        i = 0 if way > 0 else 1
        return pltpu.make_async_remote_copy(
            src_ref=a.at[sweep], dst_ref=b.at[sweep], send_sem=wsend.at[sweep, i], recv_sem=wrecv.at[sweep, i],
            device_id=to("wall", way), device_id_type=pl.DeviceIdType.MESH)

    def split_block(kind, ref, e):
        load(kind, ref, e).wait()
        for line in range(lines):
            full = wf[kind, e, line]
            high = full.astype(bf16)
            wh[kind, e, line] = high
            wl[kind, e, line] = (full - high.astype(f32)).astype(bf16)

    def pieces(x):
        high = x.astype(bf16).astype(f32)
        return jnp.concatenate([high, x - high], axis=0).astype(bf16)

    def times(x, high, low_):
        n = x.shape[0]
        both = pieces(x)
        y = jnp.dot(both, high, preferred_element_type=f32) + jnp.dot(both, low_, preferred_element_type=f32)
        return y[:n] + y[n:]

    def product(ah, al, bh, bl):
        dot = functools.partial(jnp.dot, preferred_element_type=f32)
        return dot(ah, bh) + dot(al, bh) + dot(ah, bl)

    def halves(full):
        high = full.astype(bf16)
        return high, (full - high.astype(f32)).astype(bf16)

    def form_pairs(line, unused):
        for e in range(elements):
            qh[e, line], ql[e, line] = halves(
                product(wh[0, e, line], wl[0, e, line], wh[1, e, line], wl[1, e, line]))
        return unused

    start = 1 if elements > 1 else 0

    def begin_response(line, unused):
        e = elements - 1
        th[line], tl[line] = halves(-product(wh[0, e, line], wl[0, e, line], wh[2, e, line], wl[2, e, line]))
        return unused

    def form_response(line, unused):
        eye = (lax.broadcasted_iota(jnp.int32, (width, width), 0)
               == lax.broadcasted_iota(jnp.int32, (width, width), 1)).astype(f32)
        for e in reversed(range(start, elements - 1)):
            ah, al = halves(eye - product(wh[1, e, line], wl[1, e, line], th[line], tl[line]))
            ah, al = halves(product(wh[0, e, line], wl[0, e, line], ah, al))
            th[line], tl[line] = halves(-product(ah, al, wh[2, e, line], wl[2, e, line]))
        return unused

    send_faces(0, 0)
    send_faces(0, 1)

    for axis, step, ref in (("span", 1, r_sn), ("span", -1, r_sp), ("chord", 1, r_cn), ("chord", -1, r_cp)):
        @pl.when(jnp.logical_not(has(axis, step)))
        def _():
            ref[...] = jnp.zeros_like(ref)

    @pl.when(jnp.logical_not(has("wall", -1)))
    def _():
        rf[...] = jnp.zeros_like(rf)

    @pl.when(jnp.logical_not(has("wall", 1)))
    def _():
        rb[...] = jnp.zeros_like(rb)

    ef[...] = jnp.zeros_like(ef)
    minor[0].wait()
    run = P1 * P1
    for v in range(NV):
        top = v * P1 * run
        ef[0, top:top + run, :] = face[0, v * run:(v + 1) * run, :]
        ef[0, top + 3 * run:top + 4 * run, :] = face[1, v * run:(v + 1) * run, :]
    for g in range(NV * P1):
        ef[1, g * run:g * run + P1, :] = face[2, g * P1:(g + 1) * P1, :]
        ef[1, g * run + 3 * P1:(g + 1) * run, :] = face[3, g * P1:(g + 1) * P1, :]
    for d in range(2):
        full = ef[d]
        high = full.astype(bf16)
        eh[d] = high
        el[d] = (full - high.astype(f32)).astype(bf16)

    for e in range(elements):
        split_block(0, piv, e)
        split_block(1, upp, e)

    minor[1].wait()
    minor[2].wait()

    lane = lax.broadcasted_iota(jnp.int32, (obj, width), 1)
    span_node = (lane >> 4) & 3
    chord_node = (lane >> 2) & 3

    for sweep in range(SWEEPS):
        wait_faces(sweep)
        for line in range(lines):
            for e in range(elements):
                at = (line * elements + e) * obj
                now = adj.at[0] if sweep == 0 else ab
                zs[0, at:at + obj, :] = jnp.where(
                    span_node == 0, r_sn[sweep, line, e], jnp.where(span_node == 3, r_sp[sweep, line, e], 0.0))
                above = now[line + 1, e] if line + 1 < lines else r_cn[sweep, e]
                below = now[line - 1, e] if line > 0 else r_cp[sweep, e]
                zs[1, at:at + obj, :] = jnp.where(
                    chord_node == 0, above, jnp.where(chord_node == 3, below, 0.0))
        rs[...] = times(zs[0], eh[0], el[0]) + times(zs[1], eh[1], el[1])

        last = sweep == SWEEPS - 1

        def right(line, e):
            at = (line * elements + e) * obj
            return src[0, line, e] - rs[at:at + obj, :]

        def forward(carried, final=True, first=0, end=elements):
            carried = list(carried)
            for e in range(first, end):
                for line in range(lines):
                    value = times(right(line, e) - carried[line], wh[0, e, line], wl[0, e, line])
                    fw[line, e] = value
                    if final or e < end - 1:
                        carried[line] = times(value, wh[1, e, line], wl[1, e, line])
            return carried

        def backward(carried, store, final=True, first=0, end=elements, early=True):
            carried = list(carried)
            for e in reversed(range(first, end)):
                for line in range(lines):
                    value = fw[line, e] - carried[line]
                    if store:
                        if last:
                            out[0, line, e] = value
                        else:
                            ab[line, e] = value
                    if final or e > first:
                        carried[line] = times(value, wh[2, e, line], wl[2, e, line])
                if early and store and not last and e == 1:
                    send_faces(sweep + 1, 0)
            return carried

        def received(ref):
            return [ref[sweep, line] for line in range(lines)]

        def keep(ref, values):
            for line in range(lines):
                ref[sweep, line] = values[line]

        blank = [jnp.zeros((obj, width), f32)] * lines
        opening, closing = jnp.logical_not(has("wall", -1)), jnp.logical_not(has("wall", 1))
        middle = jnp.logical_and(has("wall", -1), has("wall", 1))

        def split_lower():
            for e in reversed(range(elements)):
                split_block(2, low, e)

        @pl.when(opening)
        def _():
            if sweep == 0:
                keep(sf, forward(blank))
            else:
                carried = list(blank)
                for e in range(elements):
                    for line in range(lines):
                        small_right = right(line, e) - carried[line]
                        rs[(line * elements + e) * obj:(line * elements + e + 1) * obj, :] = small_right
                        carried[line] = times(small_right, qh[e, line], ql[e, line])
                keep(sf, carried)

            @pl.when(has("wall", 1))
            def _():
                wall_copy(sweep, 1).start()

            if sweep == 0:
                split_lower()
                lax.fori_loop(0, lines, form_pairs, 0)
            else:
                for e in range(elements):
                    for line in range(lines):
                        at = (line * elements + e) * obj
                        fw[line, e] = times(rs[at:at + obj, :], wh[0, e, line], wl[0, e, line])

            @pl.when(has("wall", 1))
            def _():
                wall_copy(sweep, -1).wait_recv()

            backward(received(rb), True, False)
            if not last:
                send_faces(sweep + 1, 1)

        @pl.when(middle)
        def _():
            if sweep == 0:
                split_lower()
            wall_copy(sweep, 1).wait_recv()
            keep(sf, forward(received(rf)))
            wall_copy(sweep, 1).start()
            wall_copy(sweep, -1).wait_recv()
            keep(sb, backward(received(rb), True))
            wall_copy(sweep, -1).start()
            if not last:
                send_faces(sweep + 1, 1)

        @pl.when(jnp.logical_and(closing, has("wall", -1)))
        def _():
            if sweep == 0:
                split_lower()
                lax.fori_loop(0, lines, begin_response, 0)
                tail = elements - 1
                forward(blank, False, tail)
                apart = backward(blank, False, True, tail)
                wall_copy(sweep, 1).wait_recv()
                came = forward(received(rf), True, 0, tail)
                back = [apart[line] + times(came[line], th[line], tl[line]) for line in range(lines)]
                keep(sb, backward(back, True, True, 0, tail, False))
                wall_copy(sweep, -1).start()
                forward(came, False, tail)
                backward(blank, True, False, tail, elements, False)
                if not last:
                    send_faces(sweep + 1, 0)
                if not last:
                    send_faces(sweep + 1, 1)
                    lax.fori_loop(0, lines, form_response, 0)
            else:
                forward(blank, False, start)
                apart = backward(blank, False, True, start)
                wall_copy(sweep, 1).wait_recv()
                came = forward(received(rf), True, 0, start)
                back = [apart[line] + times(came[line], th[line], tl[line]) for line in range(lines)]
                keep(sb, backward(back, True, True, 0, start))
                wall_copy(sweep, -1).start()
                forward(came, False, start)
                backward(blank, True, False, start)
                if not last:
                    send_faces(sweep + 1, 1)

    for sweep in range(SWEEPS):
        for part, axis, step, copy in face_copies(sweep):
            @pl.when(has(axis, step))
            def _():
                copy.wait_send()
        for way in (1, -1):
            @pl.when(has("wall", way))
            def _():
                wall_copy(sweep, way).wait_send()


def local(sizes, source, adjoint_start, pivot_inverse, upper_block, lower_block, face_coupling):
    lines, elements, obj, width = source.shape[1:]
    f32, bf16 = jnp.float32, jnp.bfloat16
    vmem = pl.BlockSpec(memory_space=pltpu.VMEM)
    anywhere = pl.BlockSpec(memory_space=pl.ANY)
    rows = lines * elements * obj
    edge = pltpu.VMEM((SWEEPS, lines, obj, width), f32)
    blocks = (3, elements, lines, width, width)
    return pl.pallas_call(
        functools.partial(kernel, sizes),
        out_shape=jax.ShapeDtypeStruct(source.shape, f32),
        in_specs=[anywhere] * 6,
        out_specs=vmem,
        scratch_shapes=[
            pltpu.VMEM(source.shape, f32), pltpu.VMEM(source.shape, f32), pltpu.VMEM(face_coupling.shape, f32),
            pltpu.VMEM(blocks[1:], bf16), pltpu.VMEM(blocks[1:], bf16),
            pltpu.VMEM(blocks[2:], bf16), pltpu.VMEM(blocks[2:], bf16), pltpu.SemaphoreType.DMA((3,)),
            pltpu.VMEM(blocks, f32), pltpu.VMEM(blocks, bf16), pltpu.VMEM(blocks, bf16),
            pltpu.VMEM((2, width, width), f32), pltpu.VMEM((2, width, width), bf16),
            pltpu.VMEM((2, width, width), bf16),
            pltpu.VMEM((2, rows, width), f32), pltpu.VMEM((rows, width), f32),
            pltpu.VMEM((lines, elements, obj, width), f32), pltpu.VMEM((lines, elements, obj, width), f32),
            edge, edge, edge, edge,
            pltpu.VMEM((SWEEPS, lines, elements, obj, width), f32),
            pltpu.VMEM((SWEEPS, lines, elements, obj, width), f32),
            pltpu.VMEM((SWEEPS, elements, obj, width), f32),
            pltpu.VMEM((SWEEPS, elements, obj, width), f32),
            pltpu.SemaphoreType.DMA((3, elements)),
            pltpu.SemaphoreType.DMA((SWEEPS, 2)), pltpu.SemaphoreType.DMA((SWEEPS, 2)),
            pltpu.SemaphoreType.DMA((SWEEPS, 2, 4)), pltpu.SemaphoreType.DMA((SWEEPS, 2, 4)),
        ],
        compiler_params=pltpu.CompilerParams(
            collective_id=0, has_side_effects=True, vmem_limit_bytes=60 * 1024 * 1024),
    )(source, adjoint_start, pivot_inverse, upper_block, lower_block, face_coupling)


def solution(mesh):
    spec = P("span", "chord", "wall", None, None)
    return jax.shard_map(
        functools.partial(local, dict(mesh.shape)),
        mesh=mesh,
        in_specs=(spec, spec, spec, spec, spec, P()),
        out_specs=spec,
        check_vma=False,
    )
```
